256 devices in a mesh: ctx: 64 (over y_lo, x, z), tp: 4 (over y_hi, core).
Axes of the slice: x: 4, y: 4 (y_hi: 2, y_lo: 2; y = y_hi * 2 + y_lo), z: 8, core: 2. Of those that a mesh axis runs over, the one named last changes fastest.
Arguments:
- tokens: bfloat16 [32768, 4096], P('ctx'), may hold values from -60 to 60
- w_query: bfloat16 [4096, 2048], P(None, 'tp'), may hold values from -0.09375 to 0.09375
- w_key: bfloat16 [4096, 512], P(None, 'tp'), may hold values from -0.09375 to 0.09375
- w_value: bfloat16 [4096, 512], P(None, 'tp'), may hold values from -0.09375 to 0.09375
- page_table: int32 [4096, 1], P('ctx'), may hold values from 0 to 63; in each aligned block of 64 rows (0 to 63, 64 to 127, ...) at most 2 rows name the same one
Outputs:
- attended: bfloat16 [32768, 2048], P('ctx', 'tp')
- kv_pool: bfloat16 [8192, 8, 2, 512], P('ctx', None, None, 'tp')
The draws below stay inside these ranges and needn't reach their ends.
Inputs may be any that keep to these rules, and one draw needn't show every extreme that they name: `page_table`: among the 64 pages of one block at most 2 have the same owner, and some owner receives exactly 2 of them.
All inputs are finite; a program needn't handle non-finite values.
Results may differ from the reference program's by a relative error of at most 0.02.
The reference program's roundings to bfloat16 on the way (of `keys_cache`, `values_cache`, `queries` and `weights`) count: a program that leaves them out, or rounds other values in their place, can miss the bound.
Values may be sent and summed in bfloat16 or wider, within the bound.
A program may use at most 128 MiB of HBM per device.

```python
import math
import jax
import jax.numpy as jnp
import numpy as np
from jax import lax

D = 4096
HD = 128
QH = 16
KVH = 4
BLK = 512
PAGE = 8
NPAGE = 64
CAP = 2
TOKENS = 32768
N_CTX = 64


def draw_tokens(key, part):
    key = jax.random.fold_in(key, 11)
    base = jax.random.normal(key, (TOKENS, D), jnp.float32)
    return jnp.clip(base, -6.0, 6.0).astype(jnp.bfloat16)


def shard_levels(stream_key, shape, split, smallest, top_value):
    factor_of = 1.0
    for dim, shards_of in split:
        heights = jax.random.uniform(jax.random.fold_in(jax.random.fold_in(stream_key, 6), dim), (shards_of,), jnp.float32, smallest / len(split), top_value / len(split))
        factor_of = factor_of * jnp.repeat(jnp.exp(heights), shape[dim] // shards_of).reshape((-1,) + (1,) * (len(shape) - 1 - dim))
    return factor_of


def routed_block(rng, own, number, rows, count, top, limit, skew):
    order = jax.random.permutation(rng, count)
    crowded, common = portions_of(count, rows * top, limit, skew, True), portions_of(count, rows * top, limit, skew, False)
    places = jnp.arange(count)

    def named(sizes, rotation):
        used = int((sizes > 0).sum())
        fixed = max(1, used // 4)
        shifted = fixed + (places - fixed + rotation * (used - fixed)) % max(1, count - fixed)
        return jnp.zeros((count,), jnp.int32).at[order[jnp.where(places < fixed, places, shifted)]].set(jnp.asarray(sizes, jnp.int32))

    sizes = jnp.where(number % 4 == 0, named(crowded, number // 4), named(common, number - number // 4 - 1))
    mixed = jax.random.permutation(jax.random.fold_in(own, 3), count)
    giver, taker = mixed[0:count // 2 * 2:2], mixed[1:count // 2 * 2:2]
    slack = jnp.minimum(sizes[giver] - 1, limit - sizes[taker]) // 2
    slack = jnp.where((giver == order[0]) | (taker == order[0]) | (sizes[taker] == 0), 0, jnp.maximum(slack, 0))
    shifted = jax.random.randint(jax.random.fold_in(own, 4), (count // 2,), 0, 1 << 20) % (slack + 1)
    sizes = sizes.at[giver].add(-shifted).at[taker].add(shifted)
    items = jnp.searchsorted(jnp.cumsum(sizes), jnp.arange(rows * top), side="right").astype(jnp.int32)
    grid = items.reshape(top, rows).T
    grid = grid[jax.random.permutation(jax.random.fold_in(own, 1), rows)]
    rotation = jax.random.randint(jax.random.fold_in(own, 2), (rows, 1), 0, top)
    return jnp.take_along_axis(grid, (jnp.arange(top)[None, :] + rotation) % top, axis=1)


def portions_of(number_of, total, limit, slope, full):
    weights = [(1 << 20) // math.isqrt(rank ** slope) + 1 for rank in range(1, number_of + 1)]
    largest = limit if full else min(limit, max(-(-total // number_of), total * weights[0] // sum(weights)))
    least = 1 if total - largest >= number_of - 1 else 0
    counts, surplus = [largest] + [least] * (number_of - 1), total - largest - least * (number_of - 1)
    while surplus > 0:
        movable = [i for i in range(1, number_of) if counts[i] < largest] or [i for i in range(1, number_of) if counts[i] < limit]
        mass, budget = sum([weights[i] for i in movable]), surplus
        for i in movable:
            extra = min(limit - counts[i], max(1, budget * weights[i] // mass), surplus)
            counts[i] = counts[i] + extra
            surplus = surplus - extra
    return np.array(counts)


def scatter_about(own_key, dims, deviation, limit, split=(), held_as=jnp.bfloat16):
    loudness = shard_levels(own_key, dims, split, -0.22, 0.18) if split else 1.0
    result = jax.random.normal(own_key, dims, jnp.float32) * deviation * loudness
    return jnp.minimum(jnp.maximum(result, -limit), limit).astype(held_as)


def setup_inputs(seed: int = 0) -> dict:
    arg_keys = jax.random.split(jax.random.key(seed), 6)
    tokens = draw_tokens(jax.random.fold_in(arg_keys[5], 71), 0)
    w_query = scatter_about(arg_keys[1], (D, QH * HD), D ** -0.5, 0.09375, ((1, 4),))
    w_key = scatter_about(arg_keys[2], (D, KVH * HD), D ** -0.5, 0.09375, ((1, 4),))
    w_value = scatter_about(arg_keys[3], (D, KVH * HD), D ** -0.5, 0.09375, ((1, 4),))
    page_table_keys = jax.random.split(jax.random.fold_in(arg_keys[4], 1), (TOKENS // PAGE) // NPAGE)
    page_table_turns = jax.random.permutation(jax.random.fold_in(arg_keys[4], 3), (TOKENS // PAGE) // NPAGE)
    page_table = jax.vmap(lambda own, number: routed_block(jax.random.fold_in(arg_keys[4], 2), own, number, NPAGE, N_CTX, 1, CAP, 2))(page_table_keys, page_table_turns).reshape((TOKENS // PAGE, 1))
    return dict(tokens=tokens, w_query=w_query, w_key=w_key, w_value=w_value, page_table=page_table)


theta_base = 500000.0
masked_value = -1e+30

def rotate(projected, positions):
    row_count = projected.shape[0]
    head_count = projected.shape[1] // HD
    split_heads = projected.reshape(row_count, head_count, HD)
    half_size = HD // 2
    frequency = theta_base ** (-(jnp.arange(half_size, dtype=jnp.float32) * 2.0 / HD))
    angles = positions[:, None] * frequency[None, :]
    cosine = jnp.cos(angles)[:, None, :]
    sine_part = jnp.sin(angles)[:, None, :]
    first_half = split_heads[..., :half_size]
    second_half = split_heads[..., half_size:]
    rotated = jnp.concatenate([first_half * cosine - second_half * sine_part, second_half * cosine + first_half * sine_part], axis=-1)
    return rotated.reshape(row_count, head_count * HD)

def attend(queries, anchor_keys, anchor_values, own_keys, own_values, block_index):
    row_count = queries.shape[0]
    kv_groups = own_keys.shape[1] // HD
    group_size = queries.shape[1] // (HD * kv_groups)
    keys_all = jnp.concatenate([anchor_keys, own_keys], 0).reshape(2 * row_count, kv_groups, HD).astype(jnp.float32)
    values_all = jnp.concatenate([anchor_values, own_values], 0).reshape(2 * row_count, kv_groups, HD).astype(jnp.float32)
    query_heads = queries.reshape(row_count, kv_groups, group_size, HD).astype(jnp.float32)
    scores = jnp.einsum('qhgd,khd->hgqk', query_heads, keys_all) / math.sqrt(HD)
    query_index = jnp.arange(row_count)[:, None]
    key_index = jnp.arange(2 * row_count)[None, :]
    visible = jnp.where(key_index < row_count, block_index > 0, key_index - row_count <= query_index)
    scores = jnp.where(visible, scores, masked_value)
    row_max = lax.optimization_barrier(jnp.max(scores, axis=-1, keepdims=True))
    weights = jnp.exp(scores - row_max)
    weights = (weights / lax.optimization_barrier(jnp.sum(weights, axis=-1, keepdims=True))).astype(jnp.bfloat16)
    mixed_heads = jnp.einsum('hgqk,khd->qhgd', weights.astype(jnp.float32), values_all)
    return mixed_heads.reshape(row_count, -1).astype(jnp.bfloat16)

def reference(tokens, w_query, w_key, w_value, page_table):
    positions_all = jnp.arange(TOKENS, dtype=jnp.float32)
    keys_cache = rotate(jnp.dot(tokens, w_key, preferred_element_type=jnp.float32), positions_all).astype(jnp.bfloat16)
    values_cache = jnp.dot(tokens, w_value, preferred_element_type=jnp.float32).astype(jnp.bfloat16)
    anchor_keys = keys_cache[:BLK]
    anchor_values = values_cache[:BLK]

    def per_block(block_index):
        first_row = (block_index * BLK).astype(jnp.int32)
        block_rows = lax.dynamic_slice_in_dim(tokens, first_row, BLK, 0)
        positions = first_row.astype(jnp.float32) + jnp.arange(BLK, dtype=jnp.float32)
        queries = rotate(jnp.dot(block_rows, w_query, preferred_element_type=jnp.float32), positions).astype(jnp.bfloat16)
        own_keys = lax.dynamic_slice_in_dim(keys_cache, first_row, BLK, 0)
        own_values = lax.dynamic_slice_in_dim(values_cache, first_row, BLK, 0)
        return attend(queries, anchor_keys, anchor_values, own_keys, own_values, block_index)
    attended = lax.map(per_block, jnp.arange(N_CTX, dtype=jnp.int32)).reshape(TOKENS, -1)
    head_width = KVH * HD
    kv_pages = jnp.stack([keys_cache.reshape(N_CTX, NPAGE, PAGE, head_width), values_cache.reshape(N_CTX, NPAGE, PAGE, head_width)], axis=3)
    owner_table = page_table.reshape(N_CTX, NPAGE)
    page_index = jnp.arange(NPAGE)
    before_mask = page_index[None, :] < page_index[:, None]
    same_owner = owner_table[:, :, None] == owner_table[:, None, :]
    page_rank = lax.optimization_barrier(jnp.sum(same_owner & before_mask[None], axis=2)).astype(jnp.int32)
    senders = jnp.arange(N_CTX, dtype=jnp.int32)[:, None]
    page_slot = (senders * CAP + page_rank).astype(jnp.int32)
    kv_pool = jnp.zeros((N_CTX, N_CTX * CAP, PAGE, 2, head_width), jnp.bfloat16).at[owner_table, page_slot].set(kv_pages)
    return (attended, kv_pool.reshape(N_CTX * N_CTX * CAP, PAGE, 2, head_width))
```

```python
import functools
import math

import jax
import jax.numpy as jnp
import numpy as np
from jax import lax
from jax.experimental import pallas as pl
from jax.experimental.pallas import tpu as pltpu
from jax.sharding import PartitionSpec as P

MESH = pl.DeviceIdType.MESH
HD = 128
BLK = 512
NPAGE = 64
PAGE = 8
CAP = 2
NZ = 8
THETA = 500000.0
SCALE = math.log2(math.e) / math.sqrt(HD)
F32 = jnp.float32
BF16 = jnp.bfloat16


def rope_tables(blocks):
    freq = THETA ** (-(np.arange(HD // 2, dtype=np.float64) * 2.0 / HD))
    freq = np.concatenate([freq, freq])
    sign = np.concatenate([-np.ones(HD // 2), np.ones(HD // 2)])
    rows = []
    for count, step in ((blocks, BLK), (BLK // 8, 8), (8, 1)):
        angle = np.arange(count)[:, None] * step * freq[None, :]
        rows += [np.cos(angle), np.sin(angle) * sign]
    return np.concatenate(rows, 0).astype(np.float32)


def kernel(
    n, chunks,
    tokens, w_query, w_key, w_value, owners, table,
    attended, pool,
    tok, wq, wkv, own, tab, placing, cosv, sinv, acc_kv, key_f, value_f, acc_q, pages, outgoing, kb, vb, qb, accl, row_max, anchor, va,
    small_sem, tok_sem, wk_sem, wv_sem, wq_sem, send_sem, recv_sem, step1_sem, step3_sem, a_sem, b_sem,
):
    me = lax.axis_index("ctx")
    z = lax.rem(me, NZ)
    q = lax.div(me, NZ)
    planes = n // NZ
    depth = tok.shape[2]
    rows = CAP * PAGE * 2

    own_copy = pltpu.make_async_copy(owners, own, small_sem.at[0])
    tab_copy = pltpu.make_async_copy(table, tab, small_sem.at[1])
    own_copy.start()
    tab_copy.start()

    def loads(i):
        k = pl.ds(pl.multiple_of(i * depth, depth), depth)
        return (
            pltpu.make_async_copy(w_key.at[k], wkv.at[i, :, pl.ds(0, HD)], wk_sem.at[i]),
            pltpu.make_async_copy(w_value.at[k], wkv.at[i, :, pl.ds(HD, HD)], wv_sem.at[i]),
            pltpu.make_async_copy(tokens.at[:, k], tok.at[i], tok_sem.at[i]),
        )

    def load_q(i):
        k = pl.ds(pl.multiple_of(i * depth, depth), depth)
        return pltpu.make_async_copy(w_query.at[k], wq.at[i], wq_sem.at[i])

    def start_loads(i, _):
        for copy in loads(i):
            copy.start()
        return 0

    def start_load_q(i, _):
        load_q(i).start()
        return 0

    lax.fori_loop(0, chunks, start_loads, 0)
    lax.fori_loop(0, chunks, start_load_q, 0)

    barrier = pltpu.get_barrier_semaphore()

    def greet(i, _):
        pl.semaphore_signal(barrier, inc=1, device_id={"ctx": lax.rem(me + i, n)}, device_id_type=MESH)
        return 0

    lax.fori_loop(1, n, greet, 0)

    own_copy.wait()
    tab_copy.wait()
    row_id = lax.broadcasted_iota(jnp.int32, (NPAGE, NPAGE), 0)
    col_id = lax.broadcasted_iota(jnp.int32, (NPAGE, NPAGE), 1)
    owner_row = own[...]
    owner_col = jnp.sum(jnp.where(row_id == col_id, owner_row, 0), axis=1, keepdims=True)
    rank = jnp.sum(jnp.where((owner_row == owner_col) & (row_id < col_id), 1, 0), axis=0, keepdims=True)
    slots = n * CAP
    slot_id = lax.broadcasted_iota(jnp.int32, (slots, NPAGE), 0)
    placing[...] = jnp.where(owner_row * CAP + rank == slot_id, 1.0, 0.0).astype(BF16)

    c1, s1 = tab[pl.ds(me, 1)], tab[pl.ds(n + me, 1)]
    base = 2 * n
    c2, s2 = tab[base : base + BLK // 8], tab[base + BLK // 8 : base + BLK // 4]
    base += BLK // 4
    c3, s3 = tab[base : base + 8], tab[base + 8 : base + 16]
    c12 = (c1 * c2 - s1 * s2).reshape(BLK // 8, 1, HD)
    s12 = (s1 * c2 + c1 * s2).reshape(BLK // 8, 1, HD)
    c3, s3 = c3.reshape(1, 8, HD), s3.reshape(1, 8, HD)
    cosv[...] = (c12 * c3 - s12 * s3).reshape(BLK, HD)
    sinv[...] = (s12 * c3 + c12 * s3).reshape(BLK, HD)
    vb[:, HD:] = jnp.ones((BLK, HD), BF16)
    va[:, HD:] = jnp.ones((BLK, HD), BF16)

    def rope(x):
        return x * cosv[...] + pltpu.roll(x, HD // 2, 1) * sinv[...]

    acc_kv[...] = jnp.zeros_like(acc_kv)

    def project_kv(i, _):
        for copy in loads(i):
            copy.wait()
        acc_kv[...] += jnp.dot(tok[i], wkv[i], preferred_element_type=F32)
        return 0

    lax.fori_loop(0, chunks, project_kv, 0)
    keys = rope(acc_kv[:, :HD])
    key_f[...] = keys
    value_f[...] = acc_kv[:, HD:]
    for t in range(PAGE):
        page_rows = pl.ds(t, NPAGE, stride=PAGE)
        part = jnp.concatenate([key_f[page_rows], value_f[page_rows]], axis=1).astype(BF16)
        placed = jnp.dot(placing[...], part, preferred_element_type=F32)
        pages[pl.ds(2 * t, slots, stride=2 * PAGE)] = placed[:, :HD]
        pages[pl.ds(2 * t + 1, slots, stride=2 * PAGE)] = placed[:, HD:]
    outgoing[...] = pages[...].astype(BF16)
    kb[...] = keys.astype(BF16)
    vb[:, :HD] = acc_kv[:, HD:].astype(BF16)

    def piece(k):
        return anchor.at[:, pl.ds(pl.multiple_of(k * (BLK // planes), BLK // planes), BLK // planes)]

    def send_piece(k, target, sems, i, recv):
        pltpu.make_async_remote_copy(
            src_ref=piece(k), dst_ref=piece(k), send_sem=sems.at[i], recv_sem=recv,
            device_id={"ctx": target}, device_id_type=MESH,
        ).start()

    pl.semaphore_wait(barrier, n - 1)

    @pl.when(me == 0)
    def _():
        anchor[0] = kb[...]
        anchor[1] = vb[:, :HD]

        def give(k, _):
            send_piece(k, k * NZ, step1_sem, k - 1, a_sem)
            return 0

        lax.fori_loop(1, planes, give, 0)

    def send_pages(i, _):
        owner = lax.rem(me + i, n)
        pltpu.make_async_remote_copy(
            src_ref=outgoing.at[pl.ds(pl.multiple_of(owner * rows, rows), rows)],
            dst_ref=pool.at[pl.ds(pl.multiple_of(me * rows, rows), rows)],
            send_sem=send_sem, recv_sem=recv_sem, device_id={"ctx": owner}, device_id_type=MESH,
        ).start()
        return 0

    lax.fori_loop(1, n, send_pages, 0)
    mine = pl.ds(pl.multiple_of(me * rows, rows), rows)
    pool[mine] = outgoing[mine]

    acc_q[...] = jnp.zeros_like(acc_q)

    def project_q(i, _):
        load_q(i).wait()
        acc_q[...] += jnp.dot(tok[i], wq[i], preferred_element_type=F32)
        return 0

    lax.fori_loop(0, chunks, project_q, 0)
    heads = acc_q.shape[1] // HD
    for h in range(heads):
        qb[h] = rope(acc_q[:, h * HD : (h + 1) * HD]).astype(BF16)

    @pl.when(me != 0)
    def _():
        pltpu.make_async_copy(piece(0), piece(0), a_sem).wait()

    @pl.when(z == 0)
    def _():
        def down(t, _):
            send_piece(q, q * NZ + t, step1_sem, planes - 1 + t - 1, a_sem)
            return 0

        lax.fori_loop(1, NZ, down, 0)

    def across(k, _):
        target = lax.rem(q + k, planes) * NZ + z

        @pl.when(target != 0)
        def _():
            send_piece(q, target, step3_sem, k - 1, b_sem)

        return 0

    lax.fori_loop(1, planes, across, 0)

    rb = BLK // 2
    nt = (((1,), (1,)), ((), ()))

    def own_part(h, _):
        for r in range(BLK // rb):
            lo, hi = r * rb, (r + 1) * rb
            s = lax.dot_general(qb[h, lo:hi], kb[:hi], nt, preferred_element_type=F32)
            query_id = lax.broadcasted_iota(jnp.int32, (rb, hi), 0) + lo
            key_id = lax.broadcasted_iota(jnp.int32, (rb, hi), 1)
            s = jnp.where(key_id <= query_id, s, -1e30)
            m = jnp.max(s, axis=1, keepdims=True)
            p = jnp.exp2((s - m) * SCALE).astype(BF16)
            accl[h, lo:hi] = jnp.dot(p, vb[:hi], preferred_element_type=F32)
            row_max[h, lo:hi] = jnp.broadcast_to(m, (rb, HD))
        return 0

    lax.fori_loop(0, heads, own_part, 0)

    @pl.when(me != 0)
    def _():
        rest = BLK - BLK // planes
        arrived = anchor.at[:, pl.ds(0, rest)]
        pltpu.make_async_copy(arrived, arrived, b_sem).wait()
        va[:, :HD] = anchor[1]

        def anchor_part(h, _):
            for r in range(BLK // rb):
                lo, hi = r * rb, (r + 1) * rb
                s = lax.dot_general(qb[h, lo:hi], anchor[0], nt, preferred_element_type=F32)
                before = row_max[h, lo:hi]
                m = jnp.maximum(before[:, :1], jnp.max(s, axis=1, keepdims=True))
                p = jnp.exp2((s - m) * SCALE).astype(BF16)
                keep = jnp.exp2((before - m) * SCALE)
                total = jnp.dot(p, va[...], preferred_element_type=F32)
                accl[h, lo:hi, :HD] = accl[h, lo:hi, :HD] * keep + total[:, :HD]
                accl[h, lo:hi, HD:] = accl[h, lo:hi, HD:] * keep + total[:, HD:]
            return 0

        lax.fori_loop(0, heads, anchor_part, 0)

    for h in range(heads):
        attended[:, h * HD : (h + 1) * HD] = (accl[h, :, :HD] / accl[h, :, HD:]).astype(BF16)

    def sent(sems, i):
        pltpu.make_async_copy(piece(0), piece(0), sems.at[i]).wait()

    @pl.when(me == 0)
    def _():
        def end(k, _):
            sent(step1_sem, k - 1)
            return 0

        lax.fori_loop(1, planes, end, 0)

    @pl.when(z == 0)
    def _():
        def end(t, _):
            sent(step1_sem, planes - 1 + t - 1)
            return 0

        lax.fori_loop(1, NZ, end, 0)

    def end3(k, _):
        @pl.when(lax.rem(q + k, planes) * NZ + z != 0)
        def _():
            sent(step3_sem, k - 1)

        return 0

    lax.fori_loop(1, planes, end3, 0)
    others = pool.at[pl.ds(0, (n - 1) * rows)]
    pltpu.make_async_copy(others, others, send_sem).wait()
    pltpu.make_async_copy(others, others, recv_sem).wait()


def hand_over(attended, pool, attended_out, pool_out, sem):
    copies = [
        pltpu.make_async_copy(attended, attended_out, sem.at[0]),
        pltpu.make_async_copy(pool, pool_out, sem.at[1]),
    ]
    for copy in copies:
        copy.start()
    for copy in copies:
        copy.wait()


def solution(mesh):
    n = mesh.shape["ctx"]
    table = rope_tables(n)

    def shards(tokens, w_query, w_key, w_value, page_table):
        width, heads = tokens.shape[1], w_query.shape[1] // HD
        chunks = 8
        depth = width // chunks
        hbm = pl.BlockSpec(memory_space=pltpu.HBM)
        vmem = pl.BlockSpec(memory_space=pltpu.VMEM)
        planes = n // NZ
        dma = pltpu.SemaphoreType.DMA
        operands = (tokens, w_query, w_key, w_value, page_table.reshape(1, NPAGE), jnp.asarray(table))
        attended, pool = pl.pallas_call(
            functools.partial(kernel, n, chunks),
            out_shape=(
                pltpu.VMEM((BLK, heads * HD), BF16),
                pltpu.VMEM((n * CAP * PAGE * 2, HD), BF16),
            ),
            in_specs=[hbm] * 6,
            out_specs=(vmem, vmem),
            scratch_shapes=[
                pltpu.VMEM((chunks, BLK, depth), BF16),
                pltpu.VMEM((chunks, depth, heads * HD), BF16),
                pltpu.VMEM((chunks, depth, 2 * HD), BF16),
                pltpu.VMEM((1, NPAGE), jnp.int32),
                pltpu.VMEM(table.shape, F32),
                pltpu.VMEM((n * CAP, NPAGE), BF16),
                pltpu.VMEM((BLK, HD), F32),
                pltpu.VMEM((BLK, HD), F32),
                pltpu.VMEM((BLK, 2 * HD), F32),
                pltpu.VMEM((BLK, HD), F32),
                pltpu.VMEM((BLK, HD), F32),
                pltpu.VMEM((BLK, heads * HD), F32),
                pltpu.VMEM((n * CAP * PAGE * 2, HD), F32),
                pltpu.VMEM((n * CAP * PAGE * 2, HD), BF16),
                pltpu.VMEM((BLK, HD), BF16),
                pltpu.VMEM((BLK, 2 * HD), BF16),
                pltpu.VMEM((heads, BLK, HD), BF16),
                pltpu.VMEM((heads, BLK, 2 * HD), F32),
                pltpu.VMEM((heads, BLK, HD), F32),
                pltpu.VMEM((2, BLK, HD), BF16),
                pltpu.VMEM((BLK, 2 * HD), BF16),
                dma((2,)),
                dma((chunks,)),
                dma((chunks,)),
                dma((chunks,)),
                dma((chunks,)),
                dma,
                dma,
                dma((planes - 1 + NZ - 1,)),
                dma((planes - 1,)),
                dma,
                dma,
            ],
            compiler_params=pltpu.CompilerParams(
                collective_id=0, has_side_effects=True, vmem_limit_bytes=48 << 20
            ),
        )(*[pltpu.with_memory_space_constraint(x, pltpu.HBM) for x in operands])
        attended, pool = pl.pallas_call(
            hand_over,
            out_shape=tuple(jax.ShapeDtypeStruct(x.shape, x.dtype) for x in (attended, pool)),
            in_specs=[vmem] * 2,
            out_specs=(hbm, hbm),
            scratch_shapes=[dma((2,))],
        )(*[pltpu.with_memory_space_constraint(x, pltpu.VMEM) for x in (attended, pool)])
        return attended, pool.reshape(n * CAP, PAGE, 2, HD)

    return jax.shard_map(
        shards,
        mesh=mesh,
        in_specs=(P("ctx", None), P(None, "tp"), P(None, "tp"), P(None, "tp"), P("ctx", None)),
        out_specs=(P("ctx", "tp"), P("ctx", None, None, "tp")),
        check_vma=False,
    )
```

```python
import functools
import math

import jax
import jax.numpy as jnp
import numpy as np
from jax import lax
from jax.experimental import pallas as pl
from jax.experimental.pallas import tpu as pltpu
from jax.sharding import PartitionSpec as P

MESH = pl.DeviceIdType.MESH
HD = 128
BLK = 512
NPAGE = 64
PAGE = 8
CAP = 2
NZ = 8
EARLY = 4
THETA = 500000.0
SCALE = math.log2(math.e) / math.sqrt(HD)
F32 = jnp.float32
BF16 = jnp.bfloat16


def rope_tables(blocks):
    freq = THETA ** (-(np.arange(HD // 2, dtype=np.float64) * 2.0 / HD))
    freq = np.concatenate([freq, freq])
    sign = np.concatenate([-np.ones(HD // 2), np.ones(HD // 2)])
    rows = []
    for count, step in ((blocks, BLK), (BLK // 8, 8), (8, 1)):
        angle = np.arange(count)[:, None] * step * freq[None, :]
        rows += [np.cos(angle), np.sin(angle) * sign]
    return np.concatenate(rows, 0).astype(np.float32)


def kernel(
    n,
    tokens, w_query, w_key, w_value, owners, table,
    attended, pool,
    tok, wq, wkv, own, tab, placing, cosv, sinv, acc_kv, key_f, value_f, acc_q, pages, outgoing, kb, vb, qb, accl, row_max, anchor, va,
    small_sem, load_sem, send_sem, recv_sem, step1_sem, step3_sem, a_sem, b_sem, here_sem, count_sem, early_sem, go_sem,
):
    me = lax.axis_index("ctx")
    z = lax.rem(me, NZ)
    q = lax.div(me, NZ)
    planes = n // NZ
    rows = CAP * PAGE * 2

    own_copy = pltpu.make_async_copy(owners, own, small_sem.at[0])
    tab_copy = pltpu.make_async_copy(table, tab, small_sem.at[1])
    own_copy.start()
    tab_copy.start()

    loads = (
        pltpu.make_async_copy(w_key, wkv.at[:, pl.ds(0, HD)], load_sem.at[0]),
        pltpu.make_async_copy(w_value, wkv.at[:, pl.ds(HD, HD)], load_sem.at[1]),
        pltpu.make_async_copy(tokens, tok, load_sem.at[2]),
    )
    load_q = pltpu.make_async_copy(w_query, wq, load_sem.at[3])
    for copy in loads:
        copy.start()

    barrier = pltpu.get_barrier_semaphore()

    def tell(sem, target):
        pl.semaphore_signal(sem, inc=1, device_id={"ctx": target}, device_id_type=MESH)

    def tell_mates(sem):
        def one(k, _):
            tell(sem, lax.rem(q + k, planes) * NZ + z)
            return 0

        lax.fori_loop(1, planes, one, 0)

    def tell_column(sem, lo, hi):
        def one(t, _):
            tell(sem, q * NZ + t)
            return 0

        lax.fori_loop(lo, hi, one, 0)

    @pl.when(z == 0)
    def _():
        tell_mates(barrier)
        pl.semaphore_wait(barrier, planes - 1)
        tell_column(barrier, 1, NZ)

    @pl.when(z != 0)
    def _():
        pl.semaphore_wait(barrier, 1)
        tell(here_sem.at[z], q * NZ)

    own_copy.wait()
    tab_copy.wait()
    row_id = lax.broadcasted_iota(jnp.int32, (NPAGE, NPAGE), 0)
    col_id = lax.broadcasted_iota(jnp.int32, (NPAGE, NPAGE), 1)
    owner_row = own[...]
    owner_col = jnp.sum(jnp.where(row_id == col_id, owner_row, 0), axis=1, keepdims=True)
    rank = jnp.sum(jnp.where((owner_row == owner_col) & (row_id < col_id), 1, 0), axis=0, keepdims=True)
    slots = n * CAP
    slot_id = lax.broadcasted_iota(jnp.int32, (slots, NPAGE), 0)
    placing[...] = jnp.where(owner_row * CAP + rank == slot_id, 1.0, 0.0).astype(BF16)

    c1, s1 = tab[pl.ds(me, 1)], tab[pl.ds(n + me, 1)]
    base = 2 * n
    c2, s2 = tab[base : base + BLK // 8], tab[base + BLK // 8 : base + BLK // 4]
    base += BLK // 4
    c3, s3 = tab[base : base + 8], tab[base + 8 : base + 16]
    c12 = (c1 * c2 - s1 * s2).reshape(BLK // 8, 1, HD)
    s12 = (s1 * c2 + c1 * s2).reshape(BLK // 8, 1, HD)
    c3, s3 = c3.reshape(1, 8, HD), s3.reshape(1, 8, HD)
    cosv[...] = (c12 * c3 - s12 * s3).reshape(BLK, HD)
    sinv[...] = (s12 * c3 + c12 * s3).reshape(BLK, HD)
    vb[:, HD:] = jnp.ones((BLK, HD), BF16)
    va[:, HD:] = jnp.ones((BLK, HD), BF16)

    def rope(x):
        return x * cosv[...] + pltpu.roll(x, HD // 2, 1) * sinv[...]

    for copy in loads:
        copy.wait()
    load_q.start()
    acc_kv[...] = jnp.dot(tok[...], wkv[...], preferred_element_type=F32)
    keys = rope(acc_kv[:, :HD])
    kb[...] = keys.astype(BF16)
    vb[:, :HD] = acc_kv[:, HD:].astype(BF16)

    def piece(k):
        return anchor.at[:, pl.ds(pl.multiple_of(k * (BLK // planes), BLK // planes), BLK // planes)]

    def send_piece(k, target, sems, i, recv):
        pltpu.make_async_remote_copy(
            src_ref=piece(k), dst_ref=piece(k), send_sem=sems.at[i], recv_sem=recv,
            device_id={"ctx": target}, device_id_type=MESH,
        ).start()

    @pl.when(me == 0)
    def _():
        anchor[0] = kb[...]
        anchor[1] = vb[:, :HD]

        def give(k, _):
            send_piece(k, k * NZ, step1_sem, k - 1, a_sem)
            return 0

        lax.fori_loop(1, planes, give, 0)

    key_f[...] = keys
    value_f[...] = acc_kv[:, HD:]
    for t in range(PAGE):
        page_rows = pl.ds(t, NPAGE, stride=PAGE)
        part = jnp.concatenate([key_f[page_rows], value_f[page_rows]], axis=1).astype(BF16)
        placed = jnp.dot(placing[...], part, preferred_element_type=F32)
        pages[pl.ds(2 * t, slots, stride=2 * PAGE)] = placed[:, :HD]
        pages[pl.ds(2 * t + 1, slots, stride=2 * PAGE)] = placed[:, HD:]
    outgoing[...] = pages[...].astype(BF16)

    mine = pl.ds(pl.multiple_of(me * rows, rows), rows)
    pool[mine] = outgoing[mine]

    def send_column(j, first, count):
        def one(t, _):
            owner = lax.rem(q + j, planes) * NZ + first + lax.rem(z + t, count)

            @pl.when(owner != me)
            def _():
                pltpu.make_async_remote_copy(
                    src_ref=outgoing.at[pl.ds(pl.multiple_of(owner * rows, rows), rows)],
                    dst_ref=pool.at[mine],
                    send_sem=send_sem, recv_sem=recv_sem, device_id={"ctx": owner}, device_id_type=MESH,
                ).start()

            return 0

        lax.fori_loop(0, count, one, 0)

    def send_planes(first, count):
        def one(j, _):
            send_column(j, first, count)
            return 0

        lax.fori_loop(0, planes, one, 0)

    def wait_piece():
        pltpu.make_async_copy(piece(0), piece(0), a_sem).wait()

    def give_mate(k):
        target = lax.rem(q + k, planes) * NZ + z

        @pl.when(target != 0)
        def _():
            send_piece(q, target, step3_sem, k - 1, b_sem)

    def share():
        def across(k, _):
            give_mate(k)
            return 0

        lax.fori_loop(1, planes, across, 0)

    def see(t, _):
        pl.semaphore_wait(here_sem.at[t], 1)
        return 0

    def down(t, _):
        send_piece(q, q * NZ + t, step1_sem, planes - 1 + t - 1, a_sem)
        return 0

    @pl.when(z >= EARLY)
    def _():
        send_planes(0, 1)
        pl.semaphore_wait(go_sem, 1)
        send_planes(1, NZ - 1)

    @pl.when((z > 0) & (z < EARLY))
    def _():
        pl.semaphore_wait(early_sem, 1)
        send_planes(0, EARLY)

    @pl.when(z == 0)
    def _():
        lax.fori_loop(1, EARLY, see, 0)
        tell_mates(count_sem.at[0])
        pl.semaphore_wait(count_sem.at[0], planes - 1)
        tell_column(early_sem, 1, EARLY)
        lax.fori_loop(EARLY, NZ, see, 0)
        tell_mates(count_sem.at[1])
        pl.semaphore_wait(count_sem.at[1], planes - 1)
        tell_column(go_sem, 1, NZ)

        @pl.when(me != 0)
        def _():
            wait_piece()

        lax.fori_loop(1, NZ, down, 0)
        share()
        send_planes(0, NZ)

    load_q.wait()
    acc_q[...] = jnp.dot(tok[...], wq[...], preferred_element_type=F32)
    heads = acc_q.shape[1] // HD
    for h in range(heads):
        qb[h] = rope(acc_q[:, h * HD : (h + 1) * HD]).astype(BF16)

    @pl.when((z > 0) & (z < EARLY))
    def _():
        wait_piece()
        share()
        pl.semaphore_wait(go_sem, 1)
        send_planes(EARLY, NZ - EARLY)

    rb = BLK // 2
    nt = (((1,), (1,)), ((), ()))

    def own_part(i, _):
        for h, r in [(2 * i + j, r) for j in range(2) for r in range(BLK // rb)]:
            lo, hi = r * rb, (r + 1) * rb
            s = lax.dot_general(qb[h, lo:hi], kb[:hi], nt, preferred_element_type=F32)
            query_id = lax.broadcasted_iota(jnp.int32, (rb, hi), 0) + lo
            key_id = lax.broadcasted_iota(jnp.int32, (rb, hi), 1)
            s = jnp.where(key_id <= query_id, s, -1e30)
            m = jnp.max(s, axis=1, keepdims=True)
            p = jnp.exp2((s - m) * SCALE).astype(BF16)
            accl[h, lo:hi] = jnp.dot(p, vb[:hi], preferred_element_type=F32)
            row_max[h, lo:hi] = jnp.broadcast_to(m, (rb, HD))
        return 0

    lax.fori_loop(0, heads // 2, own_part, 0)

    @pl.when(z >= EARLY)
    def _():
        wait_piece()
        share()

    @pl.when(me != 0)
    def _():
        rest = BLK - BLK // planes
        arrived = anchor.at[:, pl.ds(0, rest)]
        pltpu.make_async_copy(arrived, arrived, b_sem).wait()
        va[:, :HD] = anchor[1]

        def anchor_part(i, _):
            for h, r in [(2 * i + j, r) for j in range(2) for r in range(BLK // rb)]:
                lo, hi = r * rb, (r + 1) * rb
                s = lax.dot_general(qb[h, lo:hi], anchor[0], nt, preferred_element_type=F32)
                before = row_max[h, lo:hi]
                m = jnp.maximum(before[:, :1], jnp.max(s, axis=1, keepdims=True))
                p = jnp.exp2((s - m) * SCALE).astype(BF16)
                keep = jnp.exp2((before - m) * SCALE)
                total = jnp.dot(p, va[...], preferred_element_type=F32)
                accl[h, lo:hi, :HD] = accl[h, lo:hi, :HD] * keep + total[:, :HD]
                accl[h, lo:hi, HD:] = accl[h, lo:hi, HD:] * keep + total[:, HD:]
            return 0

        lax.fori_loop(0, heads // 2, anchor_part, 0)

    for h in range(heads):
        attended[:, h * HD : (h + 1) * HD] = (accl[h, :, :HD] / accl[h, :, HD:]).astype(BF16)

    def sent(sems, i):
        pltpu.make_async_copy(piece(0), piece(0), sems.at[i]).wait()

    @pl.when(me == 0)
    def _():
        def end(k, _):
            sent(step1_sem, k - 1)
            return 0

        lax.fori_loop(1, planes, end, 0)

    @pl.when(z == 0)
    def _():
        def end(t, _):
            sent(step1_sem, planes - 1 + t - 1)
            return 0

        lax.fori_loop(1, NZ, end, 0)

    def end3(k, _):
        @pl.when(lax.rem(q + k, planes) * NZ + z != 0)
        def _():
            sent(step3_sem, k - 1)

        return 0

    lax.fori_loop(1, planes, end3, 0)
    others = pool.at[pl.ds(0, (n - 1) * rows)]
    pltpu.make_async_copy(others, others, send_sem).wait()
    pltpu.make_async_copy(others, others, recv_sem).wait()


def hand_over(attended, pool, attended_out, pool_out, sem):
    copies = [
        pltpu.make_async_copy(attended, attended_out, sem.at[0]),
        pltpu.make_async_copy(pool, pool_out, sem.at[1]),
    ]
    for copy in copies:
        copy.start()
    for copy in copies:
        copy.wait()


def solution(mesh):
    n = mesh.shape["ctx"]
    table = rope_tables(n)

    def shards(tokens, w_query, w_key, w_value, page_table):
        width, heads = tokens.shape[1], w_query.shape[1] // HD
        hbm = pl.BlockSpec(memory_space=pltpu.HBM)
        vmem = pl.BlockSpec(memory_space=pltpu.VMEM)
        planes = n // NZ
        dma = pltpu.SemaphoreType.DMA
        operands = (tokens, w_query, w_key, w_value, page_table.reshape(1, NPAGE), jnp.asarray(table))
        attended, pool = pl.pallas_call(
            functools.partial(kernel, n),
            out_shape=(
                pltpu.VMEM((BLK, heads * HD), BF16),
                pltpu.VMEM((n * CAP * PAGE * 2, HD), BF16),
            ),
            in_specs=[hbm] * 6,
            out_specs=(vmem, vmem),
            scratch_shapes=[
                pltpu.VMEM((BLK, width), BF16),
                pltpu.VMEM((width, heads * HD), BF16),
                pltpu.VMEM((width, 2 * HD), BF16),
                pltpu.VMEM((1, NPAGE), jnp.int32),
                pltpu.VMEM(table.shape, F32),
                pltpu.VMEM((n * CAP, NPAGE), BF16),
                pltpu.VMEM((BLK, HD), F32),
                pltpu.VMEM((BLK, HD), F32),
                pltpu.VMEM((BLK, 2 * HD), F32),
                pltpu.VMEM((BLK, HD), F32),
                pltpu.VMEM((BLK, HD), F32),
                pltpu.VMEM((BLK, heads * HD), F32),
                pltpu.VMEM((n * CAP * PAGE * 2, HD), F32),
                pltpu.VMEM((n * CAP * PAGE * 2, HD), BF16),
                pltpu.VMEM((BLK, HD), BF16),
                pltpu.VMEM((BLK, 2 * HD), BF16),
                pltpu.VMEM((heads, BLK, HD), BF16),
                pltpu.VMEM((heads, BLK, 2 * HD), F32),
                pltpu.VMEM((heads, BLK, HD), F32),
                pltpu.VMEM((2, BLK, HD), BF16),
                pltpu.VMEM((BLK, 2 * HD), BF16),
                dma((2,)),
                dma((4,)),
                dma,
                dma,
                dma((planes - 1 + NZ - 1,)),
                dma((planes - 1,)),
                dma,
                dma,
                pltpu.SemaphoreType.REGULAR((NZ,)),
                pltpu.SemaphoreType.REGULAR((2,)),
                pltpu.SemaphoreType.REGULAR,
                pltpu.SemaphoreType.REGULAR,
            ],
            compiler_params=pltpu.CompilerParams(
                collective_id=0, has_side_effects=True, vmem_limit_bytes=48 << 20
            ),
        )(*[pltpu.with_memory_space_constraint(x, pltpu.HBM) for x in operands])
        attended, pool = pl.pallas_call(
            hand_over,
            out_shape=tuple(jax.ShapeDtypeStruct(x.shape, x.dtype) for x in (attended, pool)),
            in_specs=[vmem] * 2,
            out_specs=(hbm, hbm),
            scratch_shapes=[dma((2,))],
        )(*[pltpu.with_memory_space_constraint(x, pltpu.VMEM) for x in (attended, pool)])
        return attended, pool.reshape(n * CAP, PAGE, 2, HD)

    return jax.shard_map(
        shards,
        mesh=mesh,
        in_specs=(P("ctx", None), P(None, "tp"), P(None, "tp"), P(None, "tp"), P("ctx", None)),
        out_specs=(P("ctx", "tp"), P("ctx", None, None, "tp")),
        check_vma=False,
    )
```

```python
import functools
import math

import jax
import jax.numpy as jnp
import numpy as np
from jax import lax
from jax.experimental import pallas as pl
from jax.experimental.pallas import tpu as pltpu
from jax.sharding import PartitionSpec as P

MESH = pl.DeviceIdType.MESH
HD = 128
BLK = 512
NPAGE = 64
PAGE = 8
CAP = 2
NZ = 8
EARLY = 4
THETA = 500000.0
SCALE = math.log2(math.e) / math.sqrt(HD)
F32 = jnp.float32
BF16 = jnp.bfloat16


def rope_tables(blocks):
    freq = THETA ** (-(np.arange(HD // 2, dtype=np.float64) * 2.0 / HD))
    freq = np.concatenate([freq, freq])
    sign = np.concatenate([-np.ones(HD // 2), np.ones(HD // 2)])
    rows = []
    for count, step in ((blocks, BLK), (BLK // 8, 8), (8, 1)):
        angle = np.arange(count)[:, None] * step * freq[None, :]
        rows += [np.cos(angle), np.sin(angle) * sign]
    return np.concatenate(rows, 0).astype(np.float32)


def kernel(
    n,
    tokens, w_query, w_key, w_value, owners, table,
    attended, pool,
    tok, wq, wkv, own, tab, placing, cosv, sinv, acc_kv, key_f, value_f, acc_q, pages, outgoing, kb, vb, qb, accl, row_max, anchor, va,
    small_sem, load_sem, send_sem, recv_sem, step1_sem, step3_sem, a_sem, b_sem, here_sem, count_sem, early_sem, go_sem,
):
    me = lax.axis_index("ctx")
    z = lax.rem(me, NZ)
    q = lax.div(me, NZ)
    planes = n // NZ
    rows = CAP * PAGE * 2

    own_copy = pltpu.make_async_copy(owners, own, small_sem.at[0])
    tab_copy = pltpu.make_async_copy(table, tab, small_sem.at[1])
    own_copy.start()
    tab_copy.start()

    loads = (
        pltpu.make_async_copy(w_key, wkv.at[:, pl.ds(0, HD)], load_sem.at[0]),
        pltpu.make_async_copy(w_value, wkv.at[:, pl.ds(HD, HD)], load_sem.at[1]),
        pltpu.make_async_copy(tokens, tok, load_sem.at[2]),
    )
    load_q = pltpu.make_async_copy(w_query, wq, load_sem.at[3])
    for copy in loads:
        copy.start()

    barrier = pltpu.get_barrier_semaphore()

    def tell(sem, target):
        pl.semaphore_signal(sem, inc=1, device_id={"ctx": target}, device_id_type=MESH)

    def tell_mates(sem):
        def one(k, _):
            tell(sem, lax.rem(q + k, planes) * NZ + z)
            return 0

        lax.fori_loop(1, planes, one, 0)

    def tell_column(sem, lo, hi):
        def one(t, _):
            tell(sem, q * NZ + t)
            return 0

        lax.fori_loop(lo, hi, one, 0)

    @pl.when(z == 0)
    def _():
        tell_mates(barrier)
        pl.semaphore_wait(barrier, planes - 1)
        tell_column(barrier, 1, NZ)

    @pl.when(z != 0)
    def _():
        pl.semaphore_wait(barrier, 1)
        tell(here_sem.at[z], q * NZ)

    own_copy.wait()
    tab_copy.wait()
    row_id = lax.broadcasted_iota(jnp.int32, (NPAGE, NPAGE), 0)
    col_id = lax.broadcasted_iota(jnp.int32, (NPAGE, NPAGE), 1)
    owner_row = own[...]
    owner_col = jnp.sum(jnp.where(row_id == col_id, owner_row, 0), axis=1, keepdims=True)
    rank = jnp.sum(jnp.where((owner_row == owner_col) & (row_id < col_id), 1, 0), axis=0, keepdims=True)
    slots = n * CAP
    slot_id = lax.broadcasted_iota(jnp.int32, (slots, NPAGE), 0)
    placing[...] = jnp.where(owner_row * CAP + rank == slot_id, 1.0, 0.0).astype(BF16)

    c1, s1 = tab[pl.ds(me, 1)], tab[pl.ds(n + me, 1)]
    base = 2 * n
    c2, s2 = tab[base : base + BLK // 8], tab[base + BLK // 8 : base + BLK // 4]
    base += BLK // 4
    c3, s3 = tab[base : base + 8], tab[base + 8 : base + 16]
    c12 = (c1 * c2 - s1 * s2).reshape(BLK // 8, 1, HD)
    s12 = (s1 * c2 + c1 * s2).reshape(BLK // 8, 1, HD)
    c3, s3 = c3.reshape(1, 8, HD), s3.reshape(1, 8, HD)
    cosv[...] = (c12 * c3 - s12 * s3).reshape(BLK, HD)
    sinv[...] = (s12 * c3 + c12 * s3).reshape(BLK, HD)
    vb[:, HD:] = jnp.ones((BLK, HD), BF16)
    va[:, HD:] = jnp.ones((BLK, HD), BF16)

    def rope(x):
        return x * cosv[...] + pltpu.roll(x, HD // 2, 1) * sinv[...]

    for copy in loads:
        copy.wait()
    load_q.start()
    acc_kv[...] = jnp.dot(tok[...], wkv[...], preferred_element_type=F32)
    keys = rope(acc_kv[:, :HD])
    kb[...] = keys.astype(BF16)
    vb[:, :HD] = acc_kv[:, HD:].astype(BF16)

    def piece(k):
        return anchor.at[:, pl.ds(pl.multiple_of(k * (BLK // planes), BLK // planes), BLK // planes)]

    def send_piece(k, target, sems, i, recv):
        pltpu.make_async_remote_copy(
            src_ref=piece(k), dst_ref=piece(k), send_sem=sems.at[i], recv_sem=recv,
            device_id={"ctx": target}, device_id_type=MESH,
        ).start()

    @pl.when(me == 0)
    def _():
        anchor[0] = kb[...]
        anchor[1] = vb[:, :HD]

        def give(k, _):
            send_piece(k, k * NZ, step1_sem, k - 1, a_sem)
            return 0

        lax.fori_loop(1, planes, give, 0)

    key_f[...] = keys
    value_f[...] = acc_kv[:, HD:]
    for t in range(PAGE):
        page_rows = pl.ds(t, NPAGE, stride=PAGE)
        part = jnp.concatenate([key_f[page_rows], value_f[page_rows]], axis=1).astype(BF16)
        placed = jnp.dot(placing[...], part, preferred_element_type=F32)
        pages[pl.ds(2 * t, slots, stride=2 * PAGE)] = placed[:, :HD]
        pages[pl.ds(2 * t + 1, slots, stride=2 * PAGE)] = placed[:, HD:]
    outgoing[...] = pages[...].astype(BF16)

    mine = pl.ds(pl.multiple_of(me * rows, rows), rows)
    pool[mine] = outgoing[mine]

    def send_column(j, first, count):
        def one(t, _):
            owner = lax.rem(q + j, planes) * NZ + first + lax.rem(z + t, count)

            @pl.when(owner != me)
            def _():
                pltpu.make_async_remote_copy(
                    src_ref=outgoing.at[pl.ds(pl.multiple_of(owner * rows, rows), rows)],
                    dst_ref=pool.at[mine],
                    send_sem=send_sem, recv_sem=recv_sem, device_id={"ctx": owner}, device_id_type=MESH,
                ).start()

            return 0

        lax.fori_loop(0, count, one, 0)

    def send_planes(first, count):
        def one(j, _):
            send_column(j, first, count)
            return 0

        lax.fori_loop(0, planes, one, 0)

    def wait_piece():
        pltpu.make_async_copy(piece(0), piece(0), a_sem).wait()

    def give_mate(k):
        target = lax.rem(q + k, planes) * NZ + z

        @pl.when(target != 0)
        def _():
            send_piece(q, target, step3_sem, k - 1, b_sem)

    def share():
        def across(k, _):
            give_mate(k)
            return 0

        lax.fori_loop(1, planes, across, 0)

    def see(t, _):
        pl.semaphore_wait(here_sem.at[t], 1)
        return 0

    def see_late(t, _):
        see(t, 0)
        tell(early_sem, q * NZ + t)
        return 0

    def down(t, _):
        send_piece(q, q * NZ + t, step1_sem, planes - 1 + t - 1, a_sem)
        return 0

    @pl.when((z > 0) & (z < EARLY))
    def _():
        pl.semaphore_wait(early_sem, 1)
        send_planes(0, EARLY)

    @pl.when(z >= EARLY)
    def _():
        pl.semaphore_wait(early_sem, 1)
        send_planes(0, 2)
        pl.semaphore_wait(go_sem, 1)
        wait_piece()
        share()
        send_planes(2, EARLY - 2)

    @pl.when(z == 0)
    def _():
        lax.fori_loop(1, EARLY, see, 0)
        tell_mates(count_sem.at[0])
        pl.semaphore_wait(count_sem.at[0], planes - 1)
        tell_column(early_sem, 1, EARLY)

        @pl.when(me != 0)
        def _():
            wait_piece()

        lax.fori_loop(1, EARLY, down, 0)
        lax.fori_loop(EARLY, NZ, see_late, 0)
        tell_mates(count_sem.at[1])
        lax.fori_loop(EARLY, NZ, down, 0)
        pl.semaphore_wait(count_sem.at[1], planes - 1)
        tell_column(go_sem, 1, NZ)
        share()
        send_planes(0, NZ)

    load_q.wait()
    acc_q[...] = jnp.dot(tok[...], wq[...], preferred_element_type=F32)
    heads = acc_q.shape[1] // HD
    for h in range(heads):
        qb[h] = rope(acc_q[:, h * HD : (h + 1) * HD]).astype(BF16)

    @pl.when((z > 0) & (z < EARLY))
    def _():
        wait_piece()
        share()
        pl.semaphore_wait(go_sem, 1)
        send_planes(EARLY, NZ - EARLY)

    @pl.when(z >= EARLY)
    def _():
        send_planes(EARLY, NZ - EARLY)

    rb = BLK // 2
    nt = (((1,), (1,)), ((), ()))

    def own_part(i, _):
        for h, r in [(2 * i + j, r) for j in range(2) for r in range(BLK // rb)]:
            lo, hi = r * rb, (r + 1) * rb
            s = lax.dot_general(qb[h, lo:hi], kb[:hi], nt, preferred_element_type=F32)
            query_id = lax.broadcasted_iota(jnp.int32, (rb, hi), 0) + lo
            key_id = lax.broadcasted_iota(jnp.int32, (rb, hi), 1)
            s = jnp.where(key_id <= query_id, s, -1e30)
            m = jnp.max(s, axis=1, keepdims=True)
            p = jnp.exp2((s - m) * SCALE).astype(BF16)
            accl[h, lo:hi] = jnp.dot(p, vb[:hi], preferred_element_type=F32)
            row_max[h, lo:hi] = jnp.broadcast_to(m, (rb, HD))
        return 0

    lax.fori_loop(0, heads // 2, own_part, 0)

    @pl.when(me != 0)
    def _():
        rest = BLK - BLK // planes
        arrived = anchor.at[:, pl.ds(0, rest)]
        pltpu.make_async_copy(arrived, arrived, b_sem).wait()
        va[:, :HD] = anchor[1]

        def anchor_part(i, _):
            for h, r in [(2 * i + j, r) for j in range(2) for r in range(BLK // rb)]:
                lo, hi = r * rb, (r + 1) * rb
                s = lax.dot_general(qb[h, lo:hi], anchor[0], nt, preferred_element_type=F32)
                before = row_max[h, lo:hi]
                m = jnp.maximum(before[:, :1], jnp.max(s, axis=1, keepdims=True))
                p = jnp.exp2((s - m) * SCALE).astype(BF16)
                keep = jnp.exp2((before - m) * SCALE)
                total = jnp.dot(p, va[...], preferred_element_type=F32)
                accl[h, lo:hi, :HD] = accl[h, lo:hi, :HD] * keep + total[:, :HD]
                accl[h, lo:hi, HD:] = accl[h, lo:hi, HD:] * keep + total[:, HD:]
            return 0

        lax.fori_loop(0, heads // 2, anchor_part, 0)

    for h in range(heads):
        attended[:, h * HD : (h + 1) * HD] = (accl[h, :, :HD] / accl[h, :, HD:]).astype(BF16)

    def sent(sems, i):
        pltpu.make_async_copy(piece(0), piece(0), sems.at[i]).wait()

    @pl.when(me == 0)
    def _():
        def end(k, _):
            sent(step1_sem, k - 1)
            return 0

        lax.fori_loop(1, planes, end, 0)

    @pl.when(z == 0)
    def _():
        def end(t, _):
            sent(step1_sem, planes - 1 + t - 1)
            return 0

        lax.fori_loop(1, NZ, end, 0)

    def end3(k, _):
        @pl.when(lax.rem(q + k, planes) * NZ + z != 0)
        def _():
            sent(step3_sem, k - 1)

        return 0

    lax.fori_loop(1, planes, end3, 0)
    others = pool.at[pl.ds(0, (n - 1) * rows)]
    pltpu.make_async_copy(others, others, send_sem).wait()
    pltpu.make_async_copy(others, others, recv_sem).wait()


def hand_over(attended, pool, attended_out, pool_out, sem):
    copies = [
        pltpu.make_async_copy(attended, attended_out, sem.at[0]),
        pltpu.make_async_copy(pool, pool_out, sem.at[1]),
    ]
    for copy in copies:
        copy.start()
    for copy in copies:
        copy.wait()


def solution(mesh):
    n = mesh.shape["ctx"]
    table = rope_tables(n)

    def shards(tokens, w_query, w_key, w_value, page_table):
        width, heads = tokens.shape[1], w_query.shape[1] // HD
        hbm = pl.BlockSpec(memory_space=pltpu.HBM)
        vmem = pl.BlockSpec(memory_space=pltpu.VMEM)
        planes = n // NZ
        dma = pltpu.SemaphoreType.DMA
        operands = (tokens, w_query, w_key, w_value, page_table.reshape(1, NPAGE), jnp.asarray(table))
        attended, pool = pl.pallas_call(
            functools.partial(kernel, n),
            out_shape=(
                pltpu.VMEM((BLK, heads * HD), BF16),
                pltpu.VMEM((n * CAP * PAGE * 2, HD), BF16),
            ),
            in_specs=[hbm] * 6,
            out_specs=(vmem, vmem),
            scratch_shapes=[
                pltpu.VMEM((BLK, width), BF16),
                pltpu.VMEM((width, heads * HD), BF16),
                pltpu.VMEM((width, 2 * HD), BF16),
                pltpu.VMEM((1, NPAGE), jnp.int32),
                pltpu.VMEM(table.shape, F32),
                pltpu.VMEM((n * CAP, NPAGE), BF16),
                pltpu.VMEM((BLK, HD), F32),
                pltpu.VMEM((BLK, HD), F32),
                pltpu.VMEM((BLK, 2 * HD), F32),
                pltpu.VMEM((BLK, HD), F32),
                pltpu.VMEM((BLK, HD), F32),
                pltpu.VMEM((BLK, heads * HD), F32),
                pltpu.VMEM((n * CAP * PAGE * 2, HD), F32),
                pltpu.VMEM((n * CAP * PAGE * 2, HD), BF16),
                pltpu.VMEM((BLK, HD), BF16),
                pltpu.VMEM((BLK, 2 * HD), BF16),
                pltpu.VMEM((heads, BLK, HD), BF16),
                pltpu.VMEM((heads, BLK, 2 * HD), F32),
                pltpu.VMEM((heads, BLK, HD), F32),
                pltpu.VMEM((2, BLK, HD), BF16),
                pltpu.VMEM((BLK, 2 * HD), BF16),
                dma((2,)),
                dma((4,)),
                dma,
                dma,
                dma((planes - 1 + NZ - 1,)),
                dma((planes - 1,)),
                dma,
                dma,
                pltpu.SemaphoreType.REGULAR((NZ,)),
                pltpu.SemaphoreType.REGULAR((2,)),
                pltpu.SemaphoreType.REGULAR,
                pltpu.SemaphoreType.REGULAR,
            ],
            compiler_params=pltpu.CompilerParams(
                collective_id=0, has_side_effects=True, vmem_limit_bytes=48 << 20
            ),
        )(*[pltpu.with_memory_space_constraint(x, pltpu.HBM) for x in operands])
        attended, pool = pl.pallas_call(
            hand_over,
            out_shape=tuple(jax.ShapeDtypeStruct(x.shape, x.dtype) for x in (attended, pool)),
            in_specs=[vmem] * 2,
            out_specs=(hbm, hbm),
            scratch_shapes=[dma((2,))],
        )(*[pltpu.with_memory_space_constraint(x, pltpu.VMEM) for x in (attended, pool)])
        return attended, pool.reshape(n * CAP, PAGE, 2, HD)

    return jax.shard_map(
        shards,
        mesh=mesh,
        in_specs=(P("ctx", None), P(None, "tp"), P(None, "tp"), P(None, "tp"), P("ctx", None)),
        out_specs=(P("ctx", "tp"), P("ctx", None, None, "tp")),
        check_vma=False,
    )
```

```python
import functools
import math

import jax
import jax.numpy as jnp
import numpy as np
from jax import lax
from jax.experimental import pallas as pl
from jax.experimental.pallas import tpu as pltpu
from jax.sharding import PartitionSpec as P

MESH = pl.DeviceIdType.MESH
HD = 128
BLK = 512
NPAGE = 64
PAGE = 8
CAP = 2
NZ = 8
EARLY = 4
THETA = 500000.0
SCALE = math.log2(math.e) / math.sqrt(HD)
F32 = jnp.float32
BF16 = jnp.bfloat16


def rope_tables(blocks):
    freq = THETA ** (-(np.arange(HD // 2, dtype=np.float64) * 2.0 / HD))
    freq = np.concatenate([freq, freq])
    sign = np.concatenate([-np.ones(HD // 2), np.ones(HD // 2)])
    rows = []
    for count, step in ((blocks, BLK), (BLK // 8, 8), (8, 1)):
        angle = np.arange(count)[:, None] * step * freq[None, :]
        rows += [np.cos(angle), np.sin(angle) * sign]
    return np.concatenate(rows, 0).astype(np.float32)


def kernel(
    n,
    tokens, w_query, w_key, w_value, owners, table,
    attended, pool,
    tok, wq, wkv, own, tab, placing, cosv, sinv, acc_kv, key_f, value_f, acc_q, pages, outgoing, kb, vb, qb, accl, row_max, anchor, va,
    small_sem, load_sem, send_sem, recv_sem, step1_sem, step3_sem, a_sem, b_sem, here_sem, count_sem, early_sem, go_sem,
):
    me = lax.axis_index("ctx")
    z = lax.rem(me, NZ)
    q = lax.div(me, NZ)
    planes = n // NZ
    rows = CAP * PAGE * 2

    own_copy = pltpu.make_async_copy(owners, own, small_sem.at[0])
    tab_copy = pltpu.make_async_copy(table, tab, small_sem.at[1])
    own_copy.start()
    tab_copy.start()

    loads = (
        pltpu.make_async_copy(w_key, wkv.at[:, pl.ds(0, HD)], load_sem.at[0]),
        pltpu.make_async_copy(w_value, wkv.at[:, pl.ds(HD, HD)], load_sem.at[1]),
        pltpu.make_async_copy(tokens, tok, load_sem.at[2]),
    )
    load_q = pltpu.make_async_copy(w_query, wq, load_sem.at[3])
    for copy in loads:
        copy.start()

    barrier = pltpu.get_barrier_semaphore()

    def tell(sem, target):
        pl.semaphore_signal(sem, inc=1, device_id={"ctx": target}, device_id_type=MESH)

    def tell_mates(sem):
        def one(k, _):
            tell(sem, lax.rem(q + k, planes) * NZ + z)
            return 0

        lax.fori_loop(1, planes, one, 0)

    def tell_column(sem, lo, hi):
        def one(t, _):
            tell(sem, q * NZ + t)
            return 0

        lax.fori_loop(lo, hi, one, 0)

    def see(t, _):
        pl.semaphore_wait(here_sem.at[t], 1)
        return 0

    def see_early():
        lax.fori_loop(1, EARLY, see, 0)
        tell_mates(count_sem.at[0])

    @pl.when(z == 0)
    def _():
        tell_mates(barrier)
        pl.semaphore_wait(barrier, planes - 1)
        tell_column(barrier, 1, NZ)

        @pl.when(me != 0)
        def _():
            see_early()

    @pl.when(z != 0)
    def _():
        pl.semaphore_wait(barrier, 1)
        tell(here_sem.at[z], q * NZ)

    own_copy.wait()
    tab_copy.wait()
    row_id = lax.broadcasted_iota(jnp.int32, (NPAGE, NPAGE), 0)
    col_id = lax.broadcasted_iota(jnp.int32, (NPAGE, NPAGE), 1)
    owner_row = own[...]
    owner_col = jnp.sum(jnp.where(row_id == col_id, owner_row, 0), axis=1, keepdims=True)
    rank = jnp.sum(jnp.where((owner_row == owner_col) & (row_id < col_id), 1, 0), axis=0, keepdims=True)
    slots = n * CAP
    slot_id = lax.broadcasted_iota(jnp.int32, (slots, NPAGE), 0)
    placing[...] = jnp.where(owner_row * CAP + rank == slot_id, 1.0, 0.0).astype(BF16)

    c1, s1 = tab[pl.ds(me, 1)], tab[pl.ds(n + me, 1)]
    base = 2 * n
    c2, s2 = tab[base : base + BLK // 8], tab[base + BLK // 8 : base + BLK // 4]
    base += BLK // 4
    c3, s3 = tab[base : base + 8], tab[base + 8 : base + 16]
    c12 = (c1 * c2 - s1 * s2).reshape(BLK // 8, 1, HD)
    s12 = (s1 * c2 + c1 * s2).reshape(BLK // 8, 1, HD)
    c3, s3 = c3.reshape(1, 8, HD), s3.reshape(1, 8, HD)
    cosv[...] = (c12 * c3 - s12 * s3).reshape(BLK, HD)
    sinv[...] = (s12 * c3 + c12 * s3).reshape(BLK, HD)
    vb[:, HD:] = jnp.ones((BLK, HD), BF16)
    va[:, HD:] = jnp.ones((BLK, HD), BF16)

    def rope(x):
        return x * cosv[...] + pltpu.roll(x, HD // 2, 1) * sinv[...]

    for copy in loads:
        copy.wait()
    load_q.start()
    acc_kv[...] = jnp.dot(tok[...], wkv[...], preferred_element_type=F32)
    keys = rope(acc_kv[:, :HD])
    kb[...] = keys.astype(BF16)
    vb[:, :HD] = acc_kv[:, HD:].astype(BF16)

    def piece(k):
        return anchor.at[:, pl.ds(pl.multiple_of(k * (BLK // planes), BLK // planes), BLK // planes)]

    def send_piece(k, target, sems, i, recv):
        pltpu.make_async_remote_copy(
            src_ref=piece(k), dst_ref=piece(k), send_sem=sems.at[i], recv_sem=recv,
            device_id={"ctx": target}, device_id_type=MESH,
        ).start()

    @pl.when(me == 0)
    def _():
        anchor[0] = kb[...]
        anchor[1] = vb[:, :HD]

        def give(k, _):
            send_piece(k, k * NZ, step1_sem, k - 1, a_sem)
            return 0

        lax.fori_loop(1, planes, give, 0)
        see_early()

    key_f[...] = keys
    value_f[...] = acc_kv[:, HD:]
    for t in range(PAGE):
        page_rows = pl.ds(t, NPAGE, stride=PAGE)
        part = jnp.concatenate([key_f[page_rows], value_f[page_rows]], axis=1).astype(BF16)
        placed = jnp.dot(placing[...], part, preferred_element_type=F32)
        pages[pl.ds(2 * t, slots, stride=2 * PAGE)] = placed[:, :HD]
        pages[pl.ds(2 * t + 1, slots, stride=2 * PAGE)] = placed[:, HD:]
    outgoing[...] = pages[...].astype(BF16)

    mine = pl.ds(pl.multiple_of(me * rows, rows), rows)
    pool[mine] = outgoing[mine]

    def send_column(j, first, count):
        def one(t, _):
            owner = lax.rem(q + j, planes) * NZ + first + lax.rem(z + t, count)

            @pl.when(owner != me)
            def _():
                pltpu.make_async_remote_copy(
                    src_ref=outgoing.at[pl.ds(pl.multiple_of(owner * rows, rows), rows)],
                    dst_ref=pool.at[mine],
                    send_sem=send_sem, recv_sem=recv_sem, device_id={"ctx": owner}, device_id_type=MESH,
                ).start()

            return 0

        lax.fori_loop(0, count, one, 0)

    def send_planes(first, count):
        def one(j, _):
            send_column(j, first, count)
            return 0

        lax.fori_loop(0, planes, one, 0)

    def wait_piece():
        pltpu.make_async_copy(piece(0), piece(0), a_sem).wait()

    def give_mate(k):
        target = lax.rem(q + k, planes) * NZ + z

        @pl.when(target != 0)
        def _():
            send_piece(q, target, step3_sem, k - 1, b_sem)

    def share():
        def across(k, _):
            give_mate(k)
            return 0

        lax.fori_loop(1, planes, across, 0)

    def see_late(t, _):
        see(t, 0)
        tell(early_sem, q * NZ + t)
        return 0

    def down(t, _):
        send_piece(q, q * NZ + t, step1_sem, planes - 1 + t - 1, a_sem)
        return 0

    @pl.when((z > 0) & (z < EARLY))
    def _():
        pl.semaphore_wait(early_sem, 1)
        send_planes(0, EARLY)

    @pl.when(z >= EARLY)
    def _():
        pl.semaphore_wait(early_sem, 1)
        send_planes(0, 3)
        pl.semaphore_wait(go_sem, 1)
        wait_piece()
        share()
        send_planes(3, EARLY - 3)

    @pl.when(z == 0)
    def _():
        pl.semaphore_wait(count_sem.at[0], planes - 1)
        tell_column(early_sem, 1, EARLY)
        lax.fori_loop(EARLY, NZ, see_late, 0)
        tell_mates(count_sem.at[1])

        @pl.when(me != 0)
        def _():
            wait_piece()

        lax.fori_loop(EARLY, NZ, lambda t, _: down(NZ - 1 + EARLY - t, 0), 0)
        lax.fori_loop(1, EARLY, down, 0)
        pl.semaphore_wait(count_sem.at[1], planes - 1)
        tell_column(go_sem, 1, NZ)
        send_planes(EARLY, NZ - EARLY)
        share()
        send_planes(0, EARLY)

    load_q.wait()
    acc_q[...] = jnp.dot(tok[...], wq[...], preferred_element_type=F32)
    heads = acc_q.shape[1] // HD
    for h in range(heads):
        qb[h] = rope(acc_q[:, h * HD : (h + 1) * HD]).astype(BF16)

    @pl.when((z > 0) & (z < EARLY))
    def _():
        wait_piece()
        share()
        pl.semaphore_wait(go_sem, 1)
        send_planes(EARLY, NZ - EARLY)

    @pl.when(z >= EARLY)
    def _():
        send_planes(EARLY, NZ - EARLY)

    rb = BLK // 2
    nt = (((1,), (1,)), ((), ()))

    def own_part(i, _):
        for h, r in [(2 * i + j, r) for j in range(2) for r in range(BLK // rb)]:
            lo, hi = r * rb, (r + 1) * rb
            s = lax.dot_general(qb[h, lo:hi], kb[:hi], nt, preferred_element_type=F32)
            query_id = lax.broadcasted_iota(jnp.int32, (rb, hi), 0) + lo
            key_id = lax.broadcasted_iota(jnp.int32, (rb, hi), 1)
            s = jnp.where(key_id <= query_id, s, -1e30)
            m = jnp.max(s, axis=1, keepdims=True)
            p = jnp.exp2((s - m) * SCALE).astype(BF16)
            accl[h, lo:hi] = jnp.dot(p, vb[:hi], preferred_element_type=F32)
            row_max[h, lo:hi] = jnp.broadcast_to(m, (rb, HD))
        return 0

    lax.fori_loop(0, heads // 2, own_part, 0)

    @pl.when(me != 0)
    def _():
        rest = BLK - BLK // planes
        arrived = anchor.at[:, pl.ds(0, rest)]
        pltpu.make_async_copy(arrived, arrived, b_sem).wait()
        va[:, :HD] = anchor[1]

        def anchor_part(i, _):
            for h, r in [(2 * i + j, r) for j in range(2) for r in range(BLK // rb)]:
                lo, hi = r * rb, (r + 1) * rb
                s = lax.dot_general(qb[h, lo:hi], anchor[0], nt, preferred_element_type=F32)
                before = row_max[h, lo:hi]
                m = jnp.maximum(before[:, :1], jnp.max(s, axis=1, keepdims=True))
                p = jnp.exp2((s - m) * SCALE).astype(BF16)
                keep = jnp.exp2((before - m) * SCALE)
                total = jnp.dot(p, va[...], preferred_element_type=F32)
                top = accl[h, lo:hi, :HD] * keep + total[:, :HD]
                weight = accl[h, lo:hi, HD:] * keep + total[:, HD:]
                attended[lo:hi, pl.ds(pl.multiple_of(h * HD, HD), HD)] = (top / weight).astype(BF16)
            return 0

        lax.fori_loop(0, heads // 2, anchor_part, 0)

    @pl.when(me == 0)
    def _():
        def own_only(h, _):
            out = accl[h, :, :HD] / accl[h, :, HD:]
            attended[:, pl.ds(pl.multiple_of(h * HD, HD), HD)] = out.astype(BF16)
            return 0

        lax.fori_loop(0, heads, own_only, 0)

    def sent(sems, i):
        pltpu.make_async_copy(piece(0), piece(0), sems.at[i]).wait()

    @pl.when(me == 0)
    def _():
        def end(k, _):
            sent(step1_sem, k - 1)
            return 0

        lax.fori_loop(1, planes, end, 0)

    @pl.when(z == 0)
    def _():
        def end(t, _):
            sent(step1_sem, planes - 1 + t - 1)
            return 0

        lax.fori_loop(1, NZ, end, 0)

    def end3(k, _):
        @pl.when(lax.rem(q + k, planes) * NZ + z != 0)
        def _():
            sent(step3_sem, k - 1)

        return 0

    lax.fori_loop(1, planes, end3, 0)
    others = pool.at[pl.ds(0, (n - 1) * rows)]
    pltpu.make_async_copy(others, others, send_sem).wait()
    pltpu.make_async_copy(others, others, recv_sem).wait()


def hand_over(attended, pool, attended_out, pool_out, sem):
    copies = [
        pltpu.make_async_copy(attended, attended_out, sem.at[0]),
        pltpu.make_async_copy(pool, pool_out, sem.at[1]),
    ]
    for copy in copies:
        copy.start()
    for copy in copies:
        copy.wait()


def solution(mesh):
    n = mesh.shape["ctx"]
    table = rope_tables(n)

    def shards(tokens, w_query, w_key, w_value, page_table):
        width, heads = tokens.shape[1], w_query.shape[1] // HD
        hbm = pl.BlockSpec(memory_space=pltpu.HBM)
        vmem = pl.BlockSpec(memory_space=pltpu.VMEM)
        planes = n // NZ
        dma = pltpu.SemaphoreType.DMA
        operands = (tokens, w_query, w_key, w_value, page_table.reshape(1, NPAGE), jnp.asarray(table))
        attended, pool = pl.pallas_call(
            functools.partial(kernel, n),
            out_shape=(
                pltpu.VMEM((BLK, heads * HD), BF16),
                pltpu.VMEM((n * CAP * PAGE * 2, HD), BF16),
            ),
            in_specs=[hbm] * 6,
            out_specs=(vmem, vmem),
            scratch_shapes=[
                pltpu.VMEM((BLK, width), BF16),
                pltpu.VMEM((width, heads * HD), BF16),
                pltpu.VMEM((width, 2 * HD), BF16),
                pltpu.VMEM((1, NPAGE), jnp.int32),
                pltpu.VMEM(table.shape, F32),
                pltpu.VMEM((n * CAP, NPAGE), BF16),
                pltpu.VMEM((BLK, HD), F32),
                pltpu.VMEM((BLK, HD), F32),
                pltpu.VMEM((BLK, 2 * HD), F32),
                pltpu.VMEM((BLK, HD), F32),
                pltpu.VMEM((BLK, HD), F32),
                pltpu.VMEM((BLK, heads * HD), F32),
                pltpu.VMEM((n * CAP * PAGE * 2, HD), F32),
                pltpu.VMEM((n * CAP * PAGE * 2, HD), BF16),
                pltpu.VMEM((BLK, HD), BF16),
                pltpu.VMEM((BLK, 2 * HD), BF16),
                pltpu.VMEM((heads, BLK, HD), BF16),
                pltpu.VMEM((heads, BLK, 2 * HD), F32),
                pltpu.VMEM((heads, BLK, HD), F32),
                pltpu.VMEM((2, BLK, HD), BF16),
                pltpu.VMEM((BLK, 2 * HD), BF16),
                dma((2,)),
                dma((4,)),
                dma,
                dma,
                dma((planes - 1 + NZ - 1,)),
                dma((planes - 1,)),
                dma,
                dma,
                pltpu.SemaphoreType.REGULAR((NZ,)),
                pltpu.SemaphoreType.REGULAR((2,)),
                pltpu.SemaphoreType.REGULAR,
                pltpu.SemaphoreType.REGULAR,
            ],
            compiler_params=pltpu.CompilerParams(
                collective_id=0, has_side_effects=True, vmem_limit_bytes=48 << 20
            ),
        )(*[pltpu.with_memory_space_constraint(x, pltpu.HBM) for x in operands])
        attended, pool = pl.pallas_call(
            hand_over,
            out_shape=tuple(jax.ShapeDtypeStruct(x.shape, x.dtype) for x in (attended, pool)),
            in_specs=[vmem] * 2,
            out_specs=(hbm, hbm),
            scratch_shapes=[dma((2,))],
        )(*[pltpu.with_memory_space_constraint(x, pltpu.VMEM) for x in (attended, pool)])
        return attended, pool.reshape(n * CAP, PAGE, 2, HD)

    return jax.shard_map(
        shards,
        mesh=mesh,
        in_specs=(P("ctx", None), P(None, "tp"), P(None, "tp"), P(None, "tp"), P("ctx", None)),
        out_specs=(P("ctx", "tp"), P("ctx", None, None, "tp")),
        check_vma=False,
    )
```

```python
import functools
import math

import jax
import jax.numpy as jnp
import numpy as np
from jax import lax
from jax.experimental import pallas as pl
from jax.experimental.pallas import tpu as pltpu
from jax.sharding import PartitionSpec as P

MESH = pl.DeviceIdType.MESH
HD = 128
BLK = 512
NPAGE = 64
PAGE = 8
CAP = 2
NZ = 8
EARLY = 4
THETA = 500000.0
SCALE = math.log2(math.e) / math.sqrt(HD)
F32 = jnp.float32
BF16 = jnp.bfloat16


def rope_tables(blocks):
    freq = THETA ** (-(np.arange(HD // 2, dtype=np.float64) * 2.0 / HD))
    freq = np.concatenate([freq, freq])
    sign = np.concatenate([-np.ones(HD // 2), np.ones(HD // 2)])
    rows = []
    for count, step in ((blocks, BLK), (BLK // 8, 8), (8, 1)):
        angle = np.arange(count)[:, None] * step * freq[None, :]
        rows += [np.cos(angle), np.sin(angle) * sign]
    return np.concatenate(rows, 0).astype(np.float32)


def kernel(
    n,
    tokens, w_query, w_key, w_value, owners, table,
    attended, pool,
    tok, wq, wkv, own, tab, placing, cosv, sinv, acc_kv, key_f, value_f, acc_q, pages, outgoing, kb, vb, qb, accl, row_max, anchor, va,
    small_sem, load_sem, send_sem, recv_sem, step1_sem, step3_sem, a_sem, b_sem, here_sem, count_sem, early_sem, go_sem,
):
    me = lax.axis_index("ctx")
    z = lax.rem(me, NZ)
    q = lax.div(me, NZ)
    planes = n // NZ
    rows = CAP * PAGE * 2

    own_copy = pltpu.make_async_copy(owners, own, small_sem.at[0])
    tab_copy = pltpu.make_async_copy(table, tab, small_sem.at[1])
    own_copy.start()
    tab_copy.start()

    loads = (
        pltpu.make_async_copy(w_key, wkv.at[:, pl.ds(0, HD)], load_sem.at[0]),
        pltpu.make_async_copy(w_value, wkv.at[:, pl.ds(HD, HD)], load_sem.at[1]),
        pltpu.make_async_copy(tokens, tok, load_sem.at[2]),
    )
    load_q = pltpu.make_async_copy(w_query, wq, load_sem.at[3])
    for copy in loads:
        copy.start()

    barrier = pltpu.get_barrier_semaphore()

    def tell(sem, target):
        pl.semaphore_signal(sem, inc=1, device_id={"ctx": target}, device_id_type=MESH)

    def tell_mates(sem):
        def one(k, _):
            tell(sem, lax.rem(q + k, planes) * NZ + z)
            return 0

        lax.fori_loop(1, planes, one, 0)

    def tell_column(sem, lo, hi):
        def one(t, _):
            tell(sem, q * NZ + t)
            return 0

        lax.fori_loop(lo, hi, one, 0)

    def see(t, _):
        pl.semaphore_wait(here_sem.at[t], 1)
        return 0

    def see_early():
        lax.fori_loop(1, EARLY, see, 0)
        tell_mates(count_sem.at[0])

    @pl.when(z == 0)
    def _():
        tell_mates(barrier)
        pl.semaphore_wait(barrier, planes - 1)
        tell_column(barrier, 1, NZ)

        @pl.when(me != 0)
        def _():
            see_early()

    @pl.when(z != 0)
    def _():
        pl.semaphore_wait(barrier, 1)
        tell(here_sem.at[z], q * NZ)

    own_copy.wait()
    tab_copy.wait()
    row_id = lax.broadcasted_iota(jnp.int32, (NPAGE, NPAGE), 0)
    col_id = lax.broadcasted_iota(jnp.int32, (NPAGE, NPAGE), 1)
    owner_row = own[...]
    owner_col = jnp.sum(jnp.where(row_id == col_id, owner_row, 0), axis=1, keepdims=True)
    rank = jnp.sum(jnp.where((owner_row == owner_col) & (row_id < col_id), 1, 0), axis=0, keepdims=True)
    slots = n * CAP
    slot_id = lax.broadcasted_iota(jnp.int32, (slots, NPAGE), 0)
    placing[...] = jnp.where(owner_row * CAP + rank == slot_id, 1.0, 0.0).astype(BF16)

    c1, s1 = tab[pl.ds(me, 1)], tab[pl.ds(n + me, 1)]
    base = 2 * n
    c2, s2 = tab[base : base + BLK // 8], tab[base + BLK // 8 : base + BLK // 4]
    base += BLK // 4
    c3, s3 = tab[base : base + 8], tab[base + 8 : base + 16]
    c12 = (c1 * c2 - s1 * s2).reshape(BLK // 8, 1, HD)
    s12 = (s1 * c2 + c1 * s2).reshape(BLK // 8, 1, HD)
    c3, s3 = c3.reshape(1, 8, HD), s3.reshape(1, 8, HD)
    cosv[...] = (c12 * c3 - s12 * s3).reshape(BLK, HD)
    sinv[...] = (s12 * c3 + c12 * s3).reshape(BLK, HD)
    vb[:, HD:] = jnp.ones((BLK, HD), BF16)
    va[:, HD:] = jnp.ones((BLK, HD), BF16)

    def rope(x):
        return x * cosv[...] + pltpu.roll(x, HD // 2, 1) * sinv[...]

    for copy in loads:
        copy.wait()
    load_q.start()
    acc_kv[...] = jnp.dot(tok[...], wkv[...], preferred_element_type=F32)
    keys = rope(acc_kv[:, :HD])
    kb[...] = keys.astype(BF16)
    vb[:, :HD] = acc_kv[:, HD:].astype(BF16)

    def piece(k):
        return anchor.at[:, pl.ds(pl.multiple_of(k * (BLK // planes), BLK // planes), BLK // planes)]

    def send_piece(k, target, sems, i, recv):
        pltpu.make_async_remote_copy(
            src_ref=piece(k), dst_ref=piece(k), send_sem=sems.at[i], recv_sem=recv,
            device_id={"ctx": target}, device_id_type=MESH,
        ).start()

    @pl.when(me == 0)
    def _():
        anchor[0] = kb[...]
        anchor[1] = vb[:, :HD]

        def give(k, _):
            send_piece(k, k * NZ, step1_sem, k - 1, a_sem)
            return 0

        lax.fori_loop(1, planes, give, 0)
        see_early()

    key_f[...] = keys
    value_f[...] = acc_kv[:, HD:]
    for t in range(PAGE):
        page_rows = pl.ds(t, NPAGE, stride=PAGE)
        part = jnp.concatenate([key_f[page_rows], value_f[page_rows]], axis=1).astype(BF16)
        placed = jnp.dot(placing[...], part, preferred_element_type=F32)
        pages[pl.ds(2 * t, slots, stride=2 * PAGE)] = placed[:, :HD]
        pages[pl.ds(2 * t + 1, slots, stride=2 * PAGE)] = placed[:, HD:]
    outgoing[...] = pages[...].astype(BF16)

    mine = pl.ds(pl.multiple_of(me * rows, rows), rows)
    pool[mine] = outgoing[mine]

    def send_column(j, first, count):
        def one(t, _):
            owner = lax.rem(q + j, planes) * NZ + first + lax.rem(z + t, count)

            @pl.when(owner != me)
            def _():
                pltpu.make_async_remote_copy(
                    src_ref=outgoing.at[pl.ds(pl.multiple_of(owner * rows, rows), rows)],
                    dst_ref=pool.at[mine],
                    send_sem=send_sem, recv_sem=recv_sem, device_id={"ctx": owner}, device_id_type=MESH,
                ).start()

            return 0

        lax.fori_loop(0, count, one, 0)

    def send_planes(first, count):
        def one(j, _):
            send_column(j, first, count)
            return 0

        lax.fori_loop(0, planes, one, 0)

    def wait_piece():
        pltpu.make_async_copy(piece(0), piece(0), a_sem).wait()

    def give_mate(k):
        target = lax.rem(q + k, planes) * NZ + z

        @pl.when(target != 0)
        def _():
            send_piece(q, target, step3_sem, k - 1, b_sem)

    def share():
        def across(k, _):
            give_mate(k)
            return 0

        lax.fori_loop(1, planes, across, 0)

    def see_late(t, _):
        see(t, 0)
        tell(early_sem, q * NZ + t)
        return 0

    def down(t, _):
        send_piece(q, q * NZ + t, step1_sem, planes - 1 + t - 1, a_sem)
        return 0

    @pl.when((z > 0) & (z < EARLY))
    def _():
        pl.semaphore_wait(early_sem, 1)
        send_planes(0, EARLY)

    @pl.when(z >= EARLY)
    def _():
        pl.semaphore_wait(early_sem, 1)
        send_planes(0, 3)
        pl.semaphore_wait(go_sem, 1)
        wait_piece()
        share()
        send_planes(3, EARLY - 3)

    @pl.when(z == 0)
    def _():
        pl.semaphore_wait(count_sem.at[0], planes - 1)
        tell_column(early_sem, 1, EARLY)
        lax.fori_loop(EARLY, NZ, see_late, 0)
        tell_mates(count_sem.at[1])

        @pl.when(me != 0)
        def _():
            wait_piece()

        lax.fori_loop(EARLY, NZ, lambda t, _: down(NZ - 1 + EARLY - t, 0), 0)
        lax.fori_loop(1, EARLY, down, 0)
        pl.semaphore_wait(count_sem.at[1], planes - 1)
        tell_column(go_sem, 1, NZ)
        send_planes(EARLY, NZ - EARLY)
        share()
        send_planes(0, EARLY)

    load_q.wait()
    acc_q[...] = jnp.dot(tok[...], wq[...], preferred_element_type=F32)
    heads = acc_q.shape[1] // HD
    for h in range(heads):
        qb[h] = rope(acc_q[:, h * HD : (h + 1) * HD]).astype(BF16)

    @pl.when((z > 0) & (z < EARLY))
    def _():
        pl.semaphore_wait(go_sem, 1)
        send_planes(EARLY, NZ - EARLY)
        wait_piece()
        share()

    @pl.when(z >= EARLY)
    def _():
        send_planes(EARLY, NZ - EARLY)

    rb = BLK // 2
    nt = (((1,), (1,)), ((), ()))

    def own_part(i, _):
        for h, r in [(2 * i + j, r) for j in range(2) for r in range(BLK // rb)]:
            lo, hi = r * rb, (r + 1) * rb
            s = lax.dot_general(qb[h, lo:hi], kb[:hi], nt, preferred_element_type=F32)
            query_id = lax.broadcasted_iota(jnp.int32, (rb, hi), 0) + lo
            key_id = lax.broadcasted_iota(jnp.int32, (rb, hi), 1)
            s = jnp.where(key_id <= query_id, s, -1e30)
            m = jnp.max(s, axis=1, keepdims=True)
            p = jnp.exp2((s - m) * SCALE).astype(BF16)
            accl[h, lo:hi] = jnp.dot(p, vb[:hi], preferred_element_type=F32)
            row_max[h, lo:hi] = jnp.broadcast_to(m, (rb, HD))
        return 0

    lax.fori_loop(0, heads // 2, own_part, 0)

    @pl.when(me != 0)
    def _():
        rest = BLK - BLK // planes
        arrived = anchor.at[:, pl.ds(0, rest)]
        pltpu.make_async_copy(arrived, arrived, b_sem).wait()
        va[:, :HD] = anchor[1]

        def anchor_part(i, _):
            for h, r in [(2 * i + j, r) for j in range(2) for r in range(BLK // rb)]:
                lo, hi = r * rb, (r + 1) * rb
                s = lax.dot_general(qb[h, lo:hi], anchor[0], nt, preferred_element_type=F32)
                before = row_max[h, lo:hi]
                m = jnp.maximum(before[:, :1], jnp.max(s, axis=1, keepdims=True))
                p = jnp.exp2((s - m) * SCALE).astype(BF16)
                keep = jnp.exp2((before - m) * SCALE)
                total = jnp.dot(p, va[...], preferred_element_type=F32)
                top = accl[h, lo:hi, :HD] * keep + total[:, :HD]
                weight = accl[h, lo:hi, HD:] * keep + total[:, HD:]
                attended[lo:hi, pl.ds(pl.multiple_of(h * HD, HD), HD)] = (top / weight).astype(BF16)
            return 0

        lax.fori_loop(0, heads // 2, anchor_part, 0)

    @pl.when(me == 0)
    def _():
        def own_only(h, _):
            out = accl[h, :, :HD] / accl[h, :, HD:]
            attended[:, pl.ds(pl.multiple_of(h * HD, HD), HD)] = out.astype(BF16)
            return 0

        lax.fori_loop(0, heads, own_only, 0)

    def sent(sems, i):
        pltpu.make_async_copy(piece(0), piece(0), sems.at[i]).wait()

    @pl.when(me == 0)
    def _():
        def end(k, _):
            sent(step1_sem, k - 1)
            return 0

        lax.fori_loop(1, planes, end, 0)

    @pl.when(z == 0)
    def _():
        def end(t, _):
            sent(step1_sem, planes - 1 + t - 1)
            return 0

        lax.fori_loop(1, NZ, end, 0)

    def end3(k, _):
        @pl.when(lax.rem(q + k, planes) * NZ + z != 0)
        def _():
            sent(step3_sem, k - 1)

        return 0

    lax.fori_loop(1, planes, end3, 0)
    others = pool.at[pl.ds(0, (n - 1) * rows)]
    pltpu.make_async_copy(others, others, send_sem).wait()
    pltpu.make_async_copy(others, others, recv_sem).wait()


def hand_over(attended, pool, attended_out, pool_out, sem):
    copies = [
        pltpu.make_async_copy(attended, attended_out, sem.at[0]),
        pltpu.make_async_copy(pool, pool_out, sem.at[1]),
    ]
    for copy in copies:
        copy.start()
    for copy in copies:
        copy.wait()


def solution(mesh):
    n = mesh.shape["ctx"]
    table = rope_tables(n)

    def shards(tokens, w_query, w_key, w_value, page_table):
        width, heads = tokens.shape[1], w_query.shape[1] // HD
        hbm = pl.BlockSpec(memory_space=pltpu.HBM)
        vmem = pl.BlockSpec(memory_space=pltpu.VMEM)
        planes = n // NZ
        dma = pltpu.SemaphoreType.DMA
        operands = (tokens, w_query, w_key, w_value, page_table.reshape(1, NPAGE), jnp.asarray(table))
        attended, pool = pl.pallas_call(
            functools.partial(kernel, n),
            out_shape=(
                pltpu.VMEM((BLK, heads * HD), BF16),
                pltpu.VMEM((n * CAP * PAGE * 2, HD), BF16),
            ),
            in_specs=[hbm] * 6,
            out_specs=(vmem, vmem),
            scratch_shapes=[
                pltpu.VMEM((BLK, width), BF16),
                pltpu.VMEM((width, heads * HD), BF16),
                pltpu.VMEM((width, 2 * HD), BF16),
                pltpu.VMEM((1, NPAGE), jnp.int32),
                pltpu.VMEM(table.shape, F32),
                pltpu.VMEM((n * CAP, NPAGE), BF16),
                pltpu.VMEM((BLK, HD), F32),
                pltpu.VMEM((BLK, HD), F32),
                pltpu.VMEM((BLK, 2 * HD), F32),
                pltpu.VMEM((BLK, HD), F32),
                pltpu.VMEM((BLK, HD), F32),
                pltpu.VMEM((BLK, heads * HD), F32),
                pltpu.VMEM((n * CAP * PAGE * 2, HD), F32),
                pltpu.VMEM((n * CAP * PAGE * 2, HD), BF16),
                pltpu.VMEM((BLK, HD), BF16),
                pltpu.VMEM((BLK, 2 * HD), BF16),
                pltpu.VMEM((heads, BLK, HD), BF16),
                pltpu.VMEM((heads, BLK, 2 * HD), F32),
                pltpu.VMEM((heads, BLK, HD), F32),
                pltpu.VMEM((2, BLK, HD), BF16),
                pltpu.VMEM((BLK, 2 * HD), BF16),
                dma((2,)),
                dma((4,)),
                dma,
                dma,
                dma((planes - 1 + NZ - 1,)),
                dma((planes - 1,)),
                dma,
                dma,
                pltpu.SemaphoreType.REGULAR((NZ,)),
                pltpu.SemaphoreType.REGULAR((2,)),
                pltpu.SemaphoreType.REGULAR,
                pltpu.SemaphoreType.REGULAR,
            ],
            compiler_params=pltpu.CompilerParams(
                collective_id=0, has_side_effects=True, vmem_limit_bytes=48 << 20
            ),
        )(*[pltpu.with_memory_space_constraint(x, pltpu.HBM) for x in operands])
        attended, pool = pl.pallas_call(
            hand_over,
            out_shape=tuple(jax.ShapeDtypeStruct(x.shape, x.dtype) for x in (attended, pool)),
            in_specs=[vmem] * 2,
            out_specs=(hbm, hbm),
            scratch_shapes=[dma((2,))],
        )(*[pltpu.with_memory_space_constraint(x, pltpu.VMEM) for x in (attended, pool)])
        return attended, pool.reshape(n * CAP, PAGE, 2, HD)

    return jax.shard_map(
        shards,
        mesh=mesh,
        in_specs=(P("ctx", None), P(None, "tp"), P(None, "tp"), P(None, "tp"), P("ctx", None)),
        out_specs=(P("ctx", "tp"), P("ctx", None, None, "tp")),
        check_vma=False,
    )
```
